32 devices in a mesh: row: 4 (over y, core), col: 8 (over z, x).
Axes of the slice: x: 2, y: 2, z: 4, core: 2. Of those that a mesh axis runs over, the one named last changes fastest.
Arguments:
- tensor_tiles: bfloat16 [128, 128, 128, 128], P(('row', 'col')), may hold values from -384 to 384
- tile_mode1: int32 [128], P(('row', 'col')), may hold values from 0 to 255, as said below
- tile_mode2: int32 [128], P(('row', 'col')), may hold values from 0 to 63
- tile_mode3: int32 [128], P(('row', 'col')), may hold values from 0 to 31
- factor_mode2: bfloat16 [48, 8192], P(None, 'col'), may hold values from -1 to 1
- factor_mode3: bfloat16 [48, 4096], P(None, 'row'), may hold values from -1 to 1
Outputs:
- factor_mode1: float32 [48, 32768], P(None, ('row', 'col'))
The draws below stay inside these ranges and needn't reach their ends.
Inputs may be any that keep to these rules, and one draw needn't show every extreme that they name: `tile_mode1`: tiles at positions g*32 to (g+1)*32 - 1 have mode-1 blocks in g*64 to (g+1)*64 - 1; the 4 tiles at positions d*4 to (d+1)*4 - 1 have mode-1 blocks in distinct groups of 8 consecutive blocks (block // 8 all different).
All inputs are finite; a program needn't handle non-finite values.
Results may differ from the reference program's by a relative error of at most 0.0003.
Values may be sent and summed in bfloat16 or wider, within the bound.
A program may use at most 128 MiB of HBM per device.

```python
import jax
import jax.numpy as jnp
from jax import lax

TS = 128
R = 48
TILES_DEV = 4
IB_DEV = 8
NI = 256
NJ = 64
NK = 32
NTILES = 128
IB_ROW = 64
ROW_TILES = 32


def mixed_factor(key, row_count):
    key_noise, key_shared = jax.random.split(key)
    weight_mix = 1.0
    noise = jax.random.normal(key_noise, (R, row_count), jnp.float32)
    shared = jax.random.normal(key_shared, (row_count,), jnp.float32)
    combined = jnp.clip(noise, -4.0, 4.0) + jnp.clip(shared, -4.0, 4.0)[None, :]
    return (combined / jnp.sqrt((1.0 + weight_mix) * row_count)).astype(jnp.bfloat16)


def draw_factor_mode2(key, part):
    return mixed_factor(jax.random.fold_in(key, 2), NJ * TS)


def draw_factor_mode3(key, part):
    return mixed_factor(jax.random.fold_in(key, 3), NK * TS)


def draw_tile_mode1(key, part):
    positions = jnp.arange(NTILES, dtype=jnp.int32)
    col_count = ROW_TILES // TILES_DEV
    device_ids = positions // TILES_DEV
    within_dev = positions % TILES_DEV
    col_index = device_ids % col_count
    grid_row = device_ids // col_count
    bases = jax.random.randint(jax.random.fold_in(key, 1), (NTILES // TILES_DEV,), 0, col_count, dtype=jnp.int32)
    base_of = bases[device_ids]
    base_of = jnp.where(col_index == 0, 0, jnp.where(col_index == col_count - 1, col_count - 1, base_of))
    owners = (base_of + within_dev) % col_count
    offsets = jax.random.randint(jax.random.fold_in(key, 4), (NTILES,), 0, IB_DEV, dtype=jnp.int32)
    first_low = (within_dev == 0) & (col_index == 0)
    first_high = (within_dev == 0) & (col_index == col_count - 1)
    offsets = jnp.where(first_low, 0, jnp.where(first_high, IB_DEV - 1, offsets))
    return (grid_row * IB_ROW + owners * IB_DEV + offsets).astype(jnp.int32)


def place_ends(drawn, key, smallest, top_value):
    place = [jax.random.randint(jax.random.fold_in(key, axis), (), 0, length) for axis, length in enumerate(drawn.shape)]
    widest = drawn.shape.index(max(drawn.shape))
    beside = place[:widest] + [(place[widest] + 1) % drawn.shape[widest]] + place[widest + 1:]
    return drawn.at[tuple(place)].set(smallest).at[tuple(beside)].set(top_value)


def level_of(stream_key, extent, cuts, least, largest):
    gain, own = 1.0, jax.random.fold_in(stream_key, 6)
    for position, shards_of in cuts:
        steps = jnp.exp(jax.random.uniform(jax.random.fold_in(own, position), (shards_of,), jnp.float32, least / len(cuts), largest / len(cuts)))
        gain = gain * jnp.repeat(steps, extent[position] // shards_of).reshape([-1 if axis == position else 1 for axis in range(len(extent))])
    return gain


def centred(key, extent, spread, most, shards=(), kind=jnp.bfloat16):
    level = level_of(key, extent, shards, -0.22, 0.18) if shards else 1.0
    array = jax.random.normal(key, extent, jnp.float32) * spread * level
    return jnp.minimum(jnp.maximum(array, -most), most).astype(kind)


def setup_inputs(seed: int = 0) -> dict:
    splits = jax.random.split(jax.random.key(seed), 7)
    return {
        "tensor_tiles": centred(splits[0], (NTILES, TS, TS, TS), (0.5 * TS), 384.0, ((0, 32),)),
        "tile_mode1": draw_tile_mode1(jax.random.fold_in(splits[6], 71), 0),
        "tile_mode2": place_ends(jax.random.randint(splits[2], (NTILES,), 0, NJ), jax.random.fold_in(splits[2], 1), 0, NJ - 1).astype(jnp.int32),
        "tile_mode3": place_ends(jax.random.randint(splits[3], (NTILES,), 0, NK), jax.random.fold_in(splits[3], 1), 0, NK - 1).astype(jnp.int32),
        "factor_mode2": draw_factor_mode2(jax.random.fold_in(splits[6], 71), 0),
        "factor_mode3": draw_factor_mode3(jax.random.fold_in(splits[6], 71), 0),
    }


ridge_term = 0.5

def reference(tensor_tiles, tile_mode1, tile_mode2, tile_mode3, factor_mode2, factor_mode3):
    rank_count = factor_mode2.shape[0]
    gram_two = jnp.dot(factor_mode2.astype(jnp.float32), factor_mode2.T.astype(jnp.float32), preferred_element_type=jnp.float32)
    gram_three = jnp.dot(factor_mode3.astype(jnp.float32), factor_mode3.T.astype(jnp.float32), preferred_element_type=jnp.float32)
    system = gram_two * gram_three + ridge_term * jnp.eye(rank_count, dtype=jnp.float32)
    blocks_two = factor_mode2.reshape(rank_count, NJ, TS)
    blocks_three = factor_mode3.reshape(rank_count, NK, TS)

    def add_tile(accumulated, tile_item):
        one_tile, index_one, index_two, index_three = tile_item
        rows_two = lax.dynamic_index_in_dim(blocks_two, index_two, 1, keepdims=False).astype(jnp.float32)
        rows_three = lax.dynamic_index_in_dim(blocks_three, index_three, 1, keepdims=False).astype(jnp.float32)
        contracted = jnp.einsum('rc,abc->rab', rows_three, one_tile.astype(jnp.float32), precision=lax.Precision.HIGHEST)
        tile_rows = jnp.einsum('rab,rb->ra', contracted, rows_two, precision=lax.Precision.HIGHEST)
        column_start = (index_one * TS).astype(jnp.int32)
        anchor = jnp.zeros((), jnp.int32)
        current = lax.dynamic_slice(accumulated, (anchor, column_start), (rank_count, TS))
        return (lax.dynamic_update_slice(accumulated, current + tile_rows, (anchor, column_start)), None)
    initial = jnp.zeros((rank_count, NI * TS), jnp.float32)
    right_side, _ = lax.scan(add_tile, initial, (tensor_tiles, tile_mode1, tile_mode2, tile_mode3))
    cholesky_factor = jnp.linalg.cholesky(system)
    middle = lax.linalg.triangular_solve(cholesky_factor, right_side, left_side=True, lower=True)
    return lax.linalg.triangular_solve(cholesky_factor, middle, left_side=True, lower=True, transpose_a=True)
```

```python
import functools

import jax
import jax.numpy as jnp
from jax import lax
from jax.experimental import pallas as pl
from jax.experimental.pallas import tpu as pltpu
from jax.sharding import PartitionSpec as P

IB_DEV = 8
CORES = 2
MESH = pl.DeviceIdType.MESH
ridge_term = 0.5


def kernel(
    rows, hi, lo, chunk,
    id1, id2, id3, x_ref, f2_ref, f3_ref, out_ref,
    xv, f2g, f3g, weights, scale, sums, slots, landed,
    x_sem, own_sem, a_send, a_recv, b_send, b_recv, c_send, c_recv,
    d_send, d_recv, e_send, e_recv, s_send, s_recv,
):
    cols = hi * lo
    ny = rows // CORES
    tiles, edge = x_ref.shape[0], x_ref.shape[1]
    rank = f2_ref.shape[0]
    two_blocks = f2_ref.shape[1] // edge
    half = two_blocks // CORES
    three_blocks = f3_ref.shape[1] // edge
    me_r, me_c = lax.axis_index("row"), lax.axis_index("col")
    my_hi, my_lo = me_c // lo, lax.rem(me_c, lo)
    my_y, core = me_r // CORES, lax.rem(me_r, CORES)
    sibling = (me_r + 1 - 2 * core, me_c)

    local = []
    for ref, held, base, count in (
        (f2_ref, f2g, me_c * two_blocks, two_blocks),
        (f3_ref, f3g, me_r * three_blocks, three_blocks),
    ):
        for b in range(count):
            local.append(
                pltpu.make_async_copy(
                    ref.at[:, b * edge : (b + 1) * edge], held.at[base + b], own_sem.at[len(local)]
                )
            )
    loads = [pltpu.make_async_copy(x_ref.at[t], xv.at[t], x_sem.at[t]) for t in range(tiles)]
    for copy in local + loads:
        copy.start()

    barrier = pltpu.get_barrier_semaphore()
    partners = [(me_r, lax.rem(me_c + i, cols)) for i in range(1, cols)]
    partners.append(sibling)
    for i in range(1, ny):
        partners.append((lax.rem(my_y + i, ny) * CORES + core, me_c))
    for partner in partners:
        pl.semaphore_signal(barrier, inc=1, device_id=partner, device_id_type=MESH)
    for copy in local:
        copy.wait()
    pl.semaphore_wait(barrier, len(partners))

    sent = []

    def send(src, dst, send_sem, recv_sem, device):
        copy = pltpu.make_async_remote_copy(
            src_ref=src, dst_ref=dst, send_sem=send_sem, recv_sem=recv_sem,
            device_id=device, device_id_type=MESH,
        )
        copy.start()
        sent.append(copy)
        return copy

    def source_col(i, j):
        return lax.rem(my_hi - i + hi, hi) * lo + lax.rem(my_lo - j + lo, lo)

    def piece(col):
        return f2g.at[pl.ds(col * two_blocks + core * half, half)]

    def shard(row):
        return f3g.at[pl.ds(row * three_blocks, three_blocks)]

    mine, mine3 = piece(me_c), shard(me_r)
    a_copies, b_copies, c_copies, d_copies, e_copies = {}, {}, {}, {}, {}
    for i in range(1, hi):
        peer = (me_r, lax.rem(my_hi + i, hi) * lo + my_lo)
        a_copies[i] = send(mine, mine, a_send.at[i], a_recv.at[i], peer)

    def to_lo(i):
        where = piece(source_col(i, 0))
        for j in range(1, lo):
            peer = (me_r, my_hi * lo + lax.rem(my_lo + j, lo))
            b_copies[i, j] = send(where, where, b_send.at[i, j], b_recv.at[i, j], peer)

    def to_sibling(i, j):
        where = piece(source_col(i, j))
        c_copies[i, j] = send(where, where, c_send.at[i, j], c_recv.at[i, j], sibling)

    to_lo(0)
    for i in range(1, ny):
        peer = (lax.rem(my_y + i, ny) * CORES + core, me_c)
        e_copies[i] = send(mine3, mine3, e_send.at[i], e_recv.at[i], peer)
    d_copies[0] = send(mine3, mine3, d_send.at[0], d_recv.at[0], sibling)
    for i in range(1, hi):
        a_copies[i].wait_recv()
        to_lo(i)
        to_sibling(i, 0)
        for j in range(1, lo):
            b_copies[i - 1, j].wait_recv()
            to_sibling(i - 1, j)
    for i in range(1, ny):
        e_copies[i].wait_recv()
        where = shard(lax.rem(my_y - i + ny, ny) * CORES + core)
        d_copies[i] = send(where, where, d_send.at[i], d_recv.at[i], sibling)
    for j in range(1, lo):
        b_copies[hi - 1, j].wait_recv()
        to_sibling(hi - 1, j)
    for copy in list(c_copies.values()) + list(d_copies.values()):
        copy.wait_recv()

    for t in range(tiles):
        pair, side = t // 2, t % 2
        block = f3g[id3[t]].astype(jnp.float32)
        before = jnp.zeros((side * rank, edge), jnp.float32)
        after = jnp.zeros((edge - (side + 1) * rank, edge), jnp.float32)
        stacked = jnp.concatenate(([before] if side else []) + [block, after], axis=0)
        weights[pair, pl.ds(side * edge, edge), :] = stacked.T.astype(jnp.bfloat16)
    for pair in range(tiles // 2):
        blocks = [f2g[id2[t]].astype(jnp.float32) for t in (2 * pair, 2 * pair + 1)]
        blocks.append(jnp.zeros((edge - 2 * rank, edge), jnp.float32))
        scale[pair] = jnp.concatenate(blocks, axis=0).T

    for pair in range(tiles // 2):
        loads[2 * pair].wait()
        loads[2 * pair + 1].wait()

        def contract(step, _, pair=pair):
            at = pl.ds(pl.multiple_of(step * chunk, chunk), chunk)
            left = jnp.concatenate(
                [xv[2 * pair + s, at].reshape(chunk * edge, edge) for s in range(2)], axis=1
            )
            contracted = jnp.dot(left, weights[pair], preferred_element_type=jnp.float32)
            scaled = contracted.reshape(chunk, edge, edge) * scale[pair][None]
            sums[pair, at, :] = jnp.sum(scaled, axis=1)
            return 0

        lax.fori_loop(0, edge // chunk, contract, 0)

    tile_rows = []
    for pair in range(tiles // 2):
        turned = sums[pair].T
        tile_rows += [turned[:rank], turned[rank : 2 * rank]]
    row_blocks = IB_DEV * cols
    owners, within = [], []
    for t in range(tiles):
        block = jnp.full((rank, edge), id1[t]) - me_r * row_blocks
        owners.append(lax.div(block, jnp.int32(IB_DEV)))
        within.append(lax.rem(block[:1], jnp.int32(IB_DEV)))
    slot_copies = []
    for i in list(range(1, cols)) + [0]:
        to = lax.rem(me_c + i, cols)
        values = jnp.zeros((rank, edge), jnp.float32)
        ident = jnp.full((1, edge), -1, jnp.int32)
        for t in range(tiles):
            values = jnp.where(owners[t] == to, tile_rows[t], values)
            ident = jnp.where(owners[t][:1] == to, within[t], ident)
        target = slots if i else landed
        target[i, :rank, :] = values
        target[i, rank:, :] = jnp.broadcast_to(ident.astype(jnp.float32), (8, edge))
        if i:
            slot_copies.append(
                send(slots.at[i], landed.at[i], s_send.at[i], s_recv.at[i], (me_r, to))
            )

    nt = (((1,), (1,)), ((), ()))

    def gram(held, count):
        total = jnp.zeros((rank, rank), jnp.float32)
        for b in range(0, count, 2):
            part = jnp.concatenate([held[b], held[b + 1]], axis=1)
            total += lax.dot_general(part, part, nt, preferred_element_type=jnp.float32)
        return total

    gram_two = gram(f2g, cols * two_blocks)
    gram_three = gram(f3g, rows * three_blocks)
    row_id = lax.broadcasted_iota(jnp.int32, (rank, edge), 0)
    lane_id = lax.broadcasted_iota(jnp.int32, (rank, edge), 1)
    system = gram_two * gram_three
    padded = jnp.concatenate([system, jnp.zeros((rank, edge - rank), jnp.float32)], axis=1)
    padded = padded + jnp.where(lane_id == row_id, ridge_term, 0.0)
    start = padded + jnp.where(lane_id == row_id + rank, 1.0, 0.0)

    def eliminate(k, work):
        row = jnp.sum(jnp.where(row_id == k, work, 0.0), axis=0, keepdims=True)
        col = jnp.sum(jnp.where(lane_id == k, work, 0.0), axis=1, keepdims=True)
        pivot = jnp.sum(jnp.where(lane_id[:1] == k, row, 0.0), axis=1, keepdims=True)
        row = row / pivot
        return jnp.where(row_id == k, row, work - col * row)

    inverse = lax.fori_loop(0, rank, eliminate, start)[:, rank : 2 * rank]

    for copy in slot_copies:
        copy.wait_recv()
    for b in range(IB_DEV):
        right = jnp.zeros((rank, edge), jnp.float32)
        for i in range(cols):
            right += jnp.where(landed[i, rank : rank + 1, :] == float(b), landed[i, :rank, :], 0.0)
        out_ref[:, b * edge : (b + 1) * edge] = jnp.dot(
            inverse, right, preferred_element_type=jnp.float32, precision=lax.Precision.HIGHEST
        )
    for copy in sent:
        copy.wait_send()


def solution(mesh):
    rows, cols = mesh.shape["row"], mesh.shape["col"]
    lo = 1
    while 4 * lo * lo <= cols:
        lo *= 2
    hi = cols // lo

    def body(tensor_tiles, tile_mode1, tile_mode2, tile_mode3, factor_mode2, factor_mode3):
        tiles, edge = tensor_tiles.shape[:2]
        rank = factor_mode2.shape[0]
        two_blocks = factor_mode2.shape[1] // edge
        three_blocks = factor_mode3.shape[1] // edge
        dma = pltpu.SemaphoreType.DMA
        smem = pl.BlockSpec(memory_space=pltpu.SMEM)
        hbm = pl.BlockSpec(memory_space=pl.ANY)
        return pl.pallas_call(
            functools.partial(kernel, rows, hi, lo, 16),
            out_shape=jax.ShapeDtypeStruct((rank, IB_DEV * edge), jnp.float32),
            in_specs=[smem, smem, smem, hbm, hbm, hbm],
            out_specs=pl.BlockSpec(memory_space=pltpu.VMEM),
            scratch_shapes=[
                pltpu.VMEM(tensor_tiles.shape, jnp.bfloat16),
                pltpu.VMEM((cols * two_blocks, rank, edge), jnp.bfloat16),
                pltpu.VMEM((rows * three_blocks, rank, edge), jnp.bfloat16),
                pltpu.VMEM((tiles // 2, 2 * edge, edge), jnp.bfloat16),
                pltpu.VMEM((tiles // 2, edge, edge), jnp.float32),
                pltpu.VMEM((tiles // 2, edge, edge), jnp.float32),
                pltpu.VMEM((cols, rank + 8, edge), jnp.float32),
                pltpu.VMEM((cols, rank + 8, edge), jnp.float32),
                dma((tiles,)),
                dma((two_blocks + three_blocks,)),
                dma((hi,)), dma((hi,)),
                dma((hi, lo)), dma((hi, lo)),
                dma((hi, lo)), dma((hi, lo)),
                dma((rows,)), dma((rows,)),
                dma((rows,)), dma((rows,)),
                dma((cols,)), dma((cols,)),
            ],
            compiler_params=pltpu.CompilerParams(
                collective_id=0, has_side_effects=True, vmem_limit_bytes=48 * 1024 * 1024
            ),
        )(tile_mode1, tile_mode2, tile_mode3, tensor_tiles, factor_mode2, factor_mode3)

    in_specs = (
        P(("row", "col"), None, None, None),
        P(("row", "col")),
        P(("row", "col")),
        P(("row", "col")),
        P(None, "col"),
        P(None, "row"),
    )
    out_specs = P(None, ("row", "col"))
    return jax.shard_map(body, mesh=mesh, in_specs=in_specs, out_specs=out_specs, check_vma=False)
```

```python
import functools

import jax
import jax.numpy as jnp
from jax import lax
from jax.experimental import pallas as pl
from jax.experimental.pallas import tpu as pltpu
from jax.sharding import PartitionSpec as P

IB_DEV = 8
CORES = 2
MESH = pl.DeviceIdType.MESH
ridge_term = 0.5


def kernel(
    rows, hi, lo, chunk,
    id1_ref, id2_ref, id3_ref, x_ref, f2_ref, f3_ref, out_ref,
    id1, id2, id3, xv, f2g, f3g, weights, scale, sums, slots, landed,
    id_sem, x_sem, own_sem, a_send, a_recv, b_send, b_recv, c_send, c_recv,
    d_send, d_recv, e_send, e_recv, s_send, s_recv,
):
    cols = hi * lo
    ny = rows // CORES
    tiles, edge = x_ref.shape[0], x_ref.shape[1]
    rank = f2_ref.shape[0]
    two_blocks = f2_ref.shape[1] // edge
    half = two_blocks // CORES
    three_blocks = f3_ref.shape[1] // edge
    me_r, me_c = lax.axis_index("row"), lax.axis_index("col")
    my_hi, my_lo = me_c // lo, lax.rem(me_c, lo)
    my_y, core = me_r // CORES, lax.rem(me_r, CORES)
    sibling = (me_r + 1 - 2 * core, me_c)

    local = []
    for ref, held, base, count in (
        (f2_ref, f2g, me_c * two_blocks, two_blocks),
        (f3_ref, f3g, me_r * three_blocks, three_blocks),
    ):
        for b in range(count):
            local.append(
                pltpu.make_async_copy(
                    ref.at[:, b * edge : (b + 1) * edge], held.at[base + b], own_sem.at[len(local)]
                )
            )
    loads = [pltpu.make_async_copy(x_ref.at[t], xv.at[t], x_sem.at[t]) for t in range(tiles)]
    ids = [
        pltpu.make_async_copy(ref, held, id_sem.at[n])
        for n, (ref, held) in enumerate(((id1_ref, id1), (id2_ref, id2), (id3_ref, id3)))
    ]
    for copy in local + ids + loads:
        copy.start()

    barrier = pltpu.get_barrier_semaphore()
    partners = [(me_r, lax.rem(me_c + i, cols)) for i in range(1, cols)]
    partners.append(sibling)
    for i in range(1, ny):
        partners.append((lax.rem(my_y + i, ny) * CORES + core, me_c))
    for partner in partners:
        pl.semaphore_signal(barrier, inc=1, device_id=partner, device_id_type=MESH)
    for copy in local + ids:
        copy.wait()
    pl.semaphore_wait(barrier, len(partners))

    sent = []

    def send(src, dst, send_sem, recv_sem, device):
        copy = pltpu.make_async_remote_copy(
            src_ref=src, dst_ref=dst, send_sem=send_sem, recv_sem=recv_sem,
            device_id=device, device_id_type=MESH,
        )
        copy.start()
        sent.append(copy)
        return copy

    def source_col(i, j):
        return lax.rem(my_hi - i + hi, hi) * lo + lax.rem(my_lo - j + lo, lo)

    def piece(col):
        return f2g.at[pl.ds(col * two_blocks + core * half, half)]

    def shard(row):
        return f3g.at[pl.ds(row * three_blocks, three_blocks)]

    mine, mine3 = piece(me_c), shard(me_r)
    a_copies, b_copies, c_copies, d_copies, e_copies = {}, {}, {}, {}, {}
    for i in range(1, hi):
        peer = (me_r, lax.rem(my_hi + i, hi) * lo + my_lo)
        a_copies[i] = send(mine, mine, a_send.at[i], a_recv.at[i], peer)

    def to_lo(i):
        where = piece(source_col(i, 0))
        for j in range(1, lo):
            peer = (me_r, my_hi * lo + lax.rem(my_lo + j, lo))
            b_copies[i, j] = send(where, where, b_send.at[i, j], b_recv.at[i, j], peer)

    def to_sibling(i, j):
        where = piece(source_col(i, j))
        c_copies[i, j] = send(where, where, c_send.at[i, j], c_recv.at[i, j], sibling)

    grams = [jnp.zeros((rank, rank), jnp.float32) for _ in range(2)]

    def add_gram(which, held, base, count):
        for b in range(0, count, 2):
            part = jnp.concatenate([held[base + b], held[base + b + 1]], axis=1)
            grams[which] += lax.dot_general(
                part, part, (((1,), (1,)), ((), ())), preferred_element_type=jnp.float32
            )

    def add_piece(i, j, side):
        add_gram(0, f2g, source_col(i, j) * two_blocks + side * half, half)

    def add_shard(row):
        add_gram(1, f3g, row * three_blocks, three_blocks)

    to_lo(0)
    for i in range(1, ny):
        peer = (lax.rem(my_y + i, ny) * CORES + core, me_c)
        e_copies[i] = send(mine3, mine3, e_send.at[i], e_recv.at[i], peer)
    d_copies[0] = send(mine3, mine3, d_send.at[0], d_recv.at[0], sibling)
    add_piece(0, 0, 0)
    add_piece(0, 0, 1)
    add_shard(me_r)
    for i in range(1, hi):
        a_copies[i].wait_recv()
        to_lo(i)
        to_sibling(i, 0)
        for j in range(1, lo):
            b_copies[i - 1, j].wait_recv()
            to_sibling(i - 1, j)
        add_piece(i, 0, core)
        for j in range(1, lo):
            add_piece(i - 1, j, core)
    for i in range(1, ny):
        e_copies[i].wait_recv()
        where = shard(lax.rem(my_y - i + ny, ny) * CORES + core)
        d_copies[i] = send(where, where, d_send.at[i], d_recv.at[i], sibling)
        add_shard(lax.rem(my_y - i + ny, ny) * CORES + core)
    for j in range(1, lo):
        b_copies[hi - 1, j].wait_recv()
        to_sibling(hi - 1, j)
        add_piece(hi - 1, j, core)
    for i in range(ny):
        d_copies[i].wait_recv()
        add_shard(lax.rem(my_y - i + ny, ny) * CORES + 1 - core)
    for i, j in c_copies:
        c_copies[i, j].wait_recv()
        add_piece(i, j, 1 - core)

    for t in range(tiles):
        pair, side = t // 2, t % 2
        block = f3g[id3[t]].astype(jnp.float32)
        before = jnp.zeros((side * rank, edge), jnp.float32)
        after = jnp.zeros((edge - (side + 1) * rank, edge), jnp.float32)
        stacked = jnp.concatenate(([before] if side else []) + [block, after], axis=0)
        weights[pair, pl.ds(side * edge, edge), :] = stacked.T.astype(jnp.bfloat16)
    for pair in range(tiles // 2):
        blocks = [f2g[id2[t]].astype(jnp.float32) for t in (2 * pair, 2 * pair + 1)]
        blocks.append(jnp.zeros((edge - 2 * rank, edge), jnp.float32))
        scale[pair] = jnp.concatenate(blocks, axis=0).T

    for pair in range(tiles // 2):
        loads[2 * pair].wait()
        loads[2 * pair + 1].wait()

        def contract(step, _, pair=pair):
            at = pl.ds(pl.multiple_of(step * chunk, chunk), chunk)
            left = jnp.concatenate(
                [xv[2 * pair + s, at].reshape(chunk * edge, edge) for s in range(2)], axis=1
            )
            contracted = jnp.dot(left, weights[pair], preferred_element_type=jnp.float32)
            scaled = contracted.reshape(chunk, edge, edge) * scale[pair][None]
            sums[pair, at, :] = jnp.sum(scaled, axis=1)
            return 0

        lax.fori_loop(0, edge // chunk, contract, 0)

    tile_rows = []
    for pair in range(tiles // 2):
        turned = sums[pair].T
        tile_rows += [turned[:rank], turned[rank : 2 * rank]]
    row_blocks = IB_DEV * cols
    owners, within = [], []
    for t in range(tiles):
        block = jnp.full((rank, edge), id1[t]) - me_r * row_blocks
        owners.append(lax.div(block, jnp.int32(IB_DEV)))
        within.append(lax.rem(block[:1], jnp.int32(IB_DEV)))
    slot_copies = []
    for i in list(range(1, cols)) + [0]:
        to = lax.rem(me_c + i, cols)
        values = jnp.zeros((rank, edge), jnp.float32)
        ident = jnp.full((1, edge), -1, jnp.int32)
        for t in range(tiles):
            values = jnp.where(owners[t] == to, tile_rows[t], values)
            ident = jnp.where(owners[t][:1] == to, within[t], ident)
        target = slots if i else landed
        target[i, :rank, :] = values
        target[i, rank:, :] = jnp.broadcast_to(ident.astype(jnp.float32), (8, edge))
        if i:
            slot_copies.append(
                send(slots.at[i], landed.at[i], s_send.at[i], s_recv.at[i], (me_r, to))
            )

    row_id = lax.broadcasted_iota(jnp.int32, (rank, edge), 0)
    lane_id = lax.broadcasted_iota(jnp.int32, (rank, edge), 1)
    system = grams[0] * grams[1]
    padded = jnp.concatenate([system, jnp.zeros((rank, edge - rank), jnp.float32)], axis=1)
    padded = padded + jnp.where(lane_id == row_id, ridge_term, 0.0)
    work = padded + jnp.where(lane_id == row_id + rank, 1.0, 0.0)
    for k in range(0, rank, 2):
        first = jnp.broadcast_to(work[:, k : k + 1], (rank, edge))
        second = jnp.broadcast_to(work[:, k + 1 : k + 2], (rank, edge))
        row_a, row_b = work[k : k + 1], work[k + 1 : k + 2]
        inv_a = 1.0 / first[k : k + 1]
        cross = second[k : k + 1]
        factor = first[k + 1 : k + 2] * inv_a
        inv_b = 1.0 / (second[k + 1 : k + 2] - factor * cross)
        new_b = (row_b - factor * row_a) * inv_b
        new_a = (row_a - cross * new_b) * inv_a
        work = work - first * new_a - second * new_b
        work = jnp.where(row_id == k, new_a, jnp.where(row_id == k + 1, new_b, work))
    inverse = work[:, rank : 2 * rank]

    for copy in slot_copies:
        copy.wait_recv()
    for b in range(IB_DEV):
        right = jnp.zeros((rank, edge), jnp.float32)
        for i in range(cols):
            right += jnp.where(landed[i, rank : rank + 1, :] == float(b), landed[i, :rank, :], 0.0)
        out_ref[:, b * edge : (b + 1) * edge] = jnp.dot(
            inverse, right, preferred_element_type=jnp.float32, precision=lax.Precision.HIGHEST
        )
    for copy in sent:
        copy.wait_send()


def solution(mesh):
    rows, cols = mesh.shape["row"], mesh.shape["col"]
    lo = 1
    while 4 * lo * lo <= cols:
        lo *= 2
    hi = cols // lo

    def body(tensor_tiles, tile_mode1, tile_mode2, tile_mode3, factor_mode2, factor_mode3):
        tiles, edge = tensor_tiles.shape[:2]
        rank = factor_mode2.shape[0]
        two_blocks = factor_mode2.shape[1] // edge
        three_blocks = factor_mode3.shape[1] // edge
        dma = pltpu.SemaphoreType.DMA
        hbm = pl.BlockSpec(memory_space=pltpu.HBM)
        return pl.pallas_call(
            functools.partial(kernel, rows, hi, lo, 16),
            out_shape=jax.ShapeDtypeStruct((rank, IB_DEV * edge), jnp.float32),
            in_specs=[hbm] * 6,
            out_specs=pl.BlockSpec(memory_space=pltpu.VMEM),
            scratch_shapes=[
                pltpu.SMEM((tiles,), jnp.int32),
                pltpu.SMEM((tiles,), jnp.int32),
                pltpu.SMEM((tiles,), jnp.int32),
                pltpu.VMEM(tensor_tiles.shape, jnp.bfloat16),
                pltpu.VMEM((cols * two_blocks, rank, edge), jnp.bfloat16),
                pltpu.VMEM((rows * three_blocks, rank, edge), jnp.bfloat16),
                pltpu.VMEM((tiles // 2, 2 * edge, edge), jnp.bfloat16),
                pltpu.VMEM((tiles // 2, edge, edge), jnp.float32),
                pltpu.VMEM((tiles // 2, edge, edge), jnp.float32),
                pltpu.VMEM((cols, rank + 8, edge), jnp.float32),
                pltpu.VMEM((cols, rank + 8, edge), jnp.float32),
                dma((3,)),
                dma((tiles,)),
                dma((two_blocks + three_blocks,)),
                dma((hi,)), dma((hi,)),
                dma((hi, lo)), dma((hi, lo)),
                dma((hi, lo)), dma((hi, lo)),
                dma((rows,)), dma((rows,)),
                dma((rows,)), dma((rows,)),
                dma((cols,)), dma((cols,)),
            ],
            compiler_params=pltpu.CompilerParams(
                collective_id=0, has_side_effects=True, vmem_limit_bytes=60 * 1024 * 1024
            ),
        )(tile_mode1, tile_mode2, tile_mode3, tensor_tiles, factor_mode2, factor_mode3)

    in_specs = (
        P(("row", "col"), None, None, None),
        P(("row", "col")),
        P(("row", "col")),
        P(("row", "col")),
        P(None, "col"),
        P(None, "row"),
    )
    out_specs = P(None, ("row", "col"))
    return jax.shard_map(body, mesh=mesh, in_specs=in_specs, out_specs=out_specs, check_vma=False)
```

```python
import functools

import jax
import jax.numpy as jnp
from jax import lax
from jax.experimental import pallas as pl
from jax.experimental.pallas import tpu as pltpu
from jax.sharding import PartitionSpec as P

IB_DEV = 8
CORES = 2
MESH = pl.DeviceIdType.MESH
ridge_term = 0.5


def kernel(
    rows, hi, lo, chunk,
    id1_ref, id2_ref, id3_ref, x_ref, f2_ref, f3_ref, out_ref,
    id1, id2, id3, xv, f2g, f3g, weights, scale, sums, slots, landed,
    id_sem, x_sem, own_sem, a_send, a_recv, b_send, b_recv, c_send, c_recv,
    d_send, d_recv, e_send, e_recv, s_send, s_recv,
):
    cols = hi * lo
    ny = rows // CORES
    tiles, edge = x_ref.shape[0], x_ref.shape[1]
    rank = f2_ref.shape[0]
    two_blocks = f2_ref.shape[1] // edge
    half = two_blocks // CORES
    three_blocks = f3_ref.shape[1] // edge
    me_r, me_c = lax.axis_index("row"), lax.axis_index("col")
    my_hi, my_lo = me_c // lo, lax.rem(me_c, lo)
    my_y, core = me_r // CORES, lax.rem(me_r, CORES)
    sibling = (me_r + 1 - 2 * core, me_c)

    local = []
    for ref, held, base, count in (
        (f2_ref, f2g, me_c * two_blocks, two_blocks),
        (f3_ref, f3g, me_r * three_blocks, three_blocks),
    ):
        for b in range(count):
            local.append(
                pltpu.make_async_copy(
                    ref.at[:, b * edge : (b + 1) * edge], held.at[base + b], own_sem.at[len(local)]
                )
            )
    loads = [pltpu.make_async_copy(x_ref.at[t], xv.at[t], x_sem.at[t]) for t in range(tiles)]
    ids = [
        pltpu.make_async_copy(ref, held, id_sem.at[n])
        for n, (ref, held) in enumerate(((id1_ref, id1), (id2_ref, id2), (id3_ref, id3)))
    ]
    for copy in local + ids:
        copy.start()

    barrier = pltpu.get_barrier_semaphore()
    partners = [(me_r, lax.rem(me_c + i, cols)) for i in range(1, cols)]
    partners.append(sibling)
    for i in range(1, ny):
        partners.append((lax.rem(my_y + i, ny) * CORES + core, me_c))
    for partner in partners:
        pl.semaphore_signal(barrier, inc=1, device_id=partner, device_id_type=MESH)
    for copy in local:
        copy.wait()
    pl.semaphore_wait(barrier, len(partners))

    sent = []

    def send(src, dst, send_sem, recv_sem, device):
        copy = pltpu.make_async_remote_copy(
            src_ref=src, dst_ref=dst, send_sem=send_sem, recv_sem=recv_sem,
            device_id=device, device_id_type=MESH,
        )
        copy.start()
        sent.append(copy)
        return copy

    def source_col(i, j):
        return lax.rem(my_hi - i + hi, hi) * lo + lax.rem(my_lo - j + lo, lo)

    def piece(col):
        return f2g.at[pl.ds(col * two_blocks + core * half, half)]

    def shard(row):
        return f3g.at[pl.ds(row * three_blocks, three_blocks)]

    mine, mine3 = piece(me_c), shard(me_r)
    a_copies, b_copies, c_copies, d_copies, e_copies = {}, {}, {}, {}, {}
    for i in range(1, hi):
        peer = (me_r, lax.rem(my_hi + i, hi) * lo + my_lo)
        a_copies[i] = send(mine, mine, a_send.at[i], a_recv.at[i], peer)

    def to_lo(i):
        where = piece(source_col(i, 0))
        for j in range(1, lo):
            peer = (me_r, my_hi * lo + lax.rem(my_lo + j, lo))
            b_copies[i, j] = send(where, where, b_send.at[i, j], b_recv.at[i, j], peer)

    def to_sibling(i, j):
        where = piece(source_col(i, j))
        c_copies[i, j] = send(where, where, c_send.at[i, j], c_recv.at[i, j], sibling)

    to_lo(0)
    for i in range(1, ny):
        peer = (lax.rem(my_y + i, ny) * CORES + core, me_c)
        e_copies[i] = send(mine3, mine3, e_send.at[i], e_recv.at[i], peer)
    d_copies[0] = send(mine3, mine3, d_send.at[0], d_recv.at[0], sibling)
    for copy in loads:
        copy.start()
    for i in range(1, hi):
        a_copies[i].wait_recv()
        to_lo(i)
        to_sibling(i, 0)
        for j in range(1, lo):
            b_copies[i - 1, j].wait_recv()
            to_sibling(i - 1, j)
    for i in range(1, ny):
        e_copies[i].wait_recv()
        where = shard(lax.rem(my_y - i + ny, ny) * CORES + core)
        d_copies[i] = send(where, where, d_send.at[i], d_recv.at[i], sibling)
    for j in range(1, lo):
        b_copies[hi - 1, j].wait_recv()
        to_sibling(hi - 1, j)
    for copy in list(c_copies.values()) + list(d_copies.values()):
        copy.wait_recv()
    for copy in ids:
        copy.wait()

    for t in range(tiles):
        pair, side = t // 2, t % 2
        block = f3g[id3[t]].astype(jnp.float32)
        before = jnp.zeros((side * rank, edge), jnp.float32)
        after = jnp.zeros((edge - (side + 1) * rank, edge), jnp.float32)
        stacked = jnp.concatenate(([before] if side else []) + [block, after], axis=0)
        weights[pair, pl.ds(side * edge, edge), :] = stacked.T.astype(jnp.bfloat16)
    for pair in range(tiles // 2):
        blocks = [f2g[id2[t]].astype(jnp.float32) for t in (2 * pair, 2 * pair + 1)]
        blocks.append(jnp.zeros((edge - 2 * rank, edge), jnp.float32))
        scale[pair] = jnp.concatenate(blocks, axis=0).T

    for pair in range(tiles // 2):
        loads[2 * pair].wait()
        loads[2 * pair + 1].wait()

        def contract(step, _, pair=pair):
            at = pl.ds(pl.multiple_of(step * chunk, chunk), chunk)
            left = jnp.concatenate(
                [xv[2 * pair + s, at].reshape(chunk * edge, edge) for s in range(2)], axis=1
            )
            contracted = jnp.dot(left, weights[pair], preferred_element_type=jnp.float32)
            scaled = contracted.reshape(chunk, edge, edge) * scale[pair][None]
            sums[pair, at, :] = jnp.sum(scaled, axis=1)
            return 0

        lax.fori_loop(0, edge // chunk, contract, 0)

    tile_rows = []
    for pair in range(tiles // 2):
        turned = sums[pair].T
        tile_rows += [turned[:rank], turned[rank : 2 * rank]]
    row_blocks = IB_DEV * cols
    owners, within = [], []
    for t in range(tiles):
        block = jnp.full((rank, edge), id1[t]) - me_r * row_blocks
        owners.append(lax.div(block, jnp.int32(IB_DEV)))
        within.append(lax.rem(block[:1], jnp.int32(IB_DEV)))
    slot_copies = []
    for i in list(range(1, cols)) + [0]:
        to = lax.rem(me_c + i, cols)
        values = jnp.zeros((rank, edge), jnp.float32)
        ident = jnp.full((1, edge), -1, jnp.int32)
        for t in range(tiles):
            values = jnp.where(owners[t] == to, tile_rows[t], values)
            ident = jnp.where(owners[t][:1] == to, within[t], ident)
        target = slots if i else landed
        target[i, :rank, :] = values
        target[i, rank:, :] = jnp.broadcast_to(ident.astype(jnp.float32), (8, edge))
        if i:
            slot_copies.append(
                send(slots.at[i], landed.at[i], s_send.at[i], s_recv.at[i], (me_r, to))
            )

    def gram(held, count):
        total = jnp.zeros((rank, rank), jnp.float32)
        for base in range(0, count, 16):
            part = jnp.concatenate([held[b] for b in range(base, min(base + 16, count))], axis=1)
            total += lax.dot_general(
                part, part, (((1,), (1,)), ((), ())), preferred_element_type=jnp.float32
            )
        return total

    row_id = lax.broadcasted_iota(jnp.int32, (rank, edge), 0)
    lane_id = lax.broadcasted_iota(jnp.int32, (rank, edge), 1)
    system = gram(f2g, cols * two_blocks) * gram(f3g, rows * three_blocks)
    padded = jnp.concatenate([system, jnp.zeros((rank, edge - rank), jnp.float32)], axis=1)
    padded = padded + jnp.where(lane_id == row_id, ridge_term, 0.0)
    work = padded + jnp.where(lane_id == row_id + rank, 1.0, 0.0)
    for k in range(0, rank, 2):
        first = jnp.broadcast_to(work[:, k : k + 1], (rank, edge))
        second = jnp.broadcast_to(work[:, k + 1 : k + 2], (rank, edge))
        row_a, row_b = work[k : k + 1], work[k + 1 : k + 2]
        inv_a = 1.0 / first[k : k + 1]
        cross = second[k : k + 1]
        factor = first[k + 1 : k + 2] * inv_a
        inv_b = 1.0 / (second[k + 1 : k + 2] - factor * cross)
        new_b = (row_b - factor * row_a) * inv_b
        new_a = (row_a - cross * new_b) * inv_a
        work = work - first * new_a - second * new_b
        work = jnp.where(row_id == k, new_a, jnp.where(row_id == k + 1, new_b, work))
    inverse = work[:, rank : 2 * rank]

    for copy in slot_copies:
        copy.wait_recv()
    for b in range(IB_DEV):
        right = jnp.zeros((rank, edge), jnp.float32)
        for i in range(cols):
            right += jnp.where(landed[i, rank : rank + 1, :] == float(b), landed[i, :rank, :], 0.0)
        out_ref[:, b * edge : (b + 1) * edge] = jnp.dot(
            inverse, right, preferred_element_type=jnp.float32, precision=lax.Precision.HIGHEST
        )
    for copy in sent:
        copy.wait_send()


def solution(mesh):
    rows, cols = mesh.shape["row"], mesh.shape["col"]
    lo = 1
    while 4 * lo * lo <= cols:
        lo *= 2
    hi = cols // lo

    def body(tensor_tiles, tile_mode1, tile_mode2, tile_mode3, factor_mode2, factor_mode3):
        tiles, edge = tensor_tiles.shape[:2]
        rank = factor_mode2.shape[0]
        two_blocks = factor_mode2.shape[1] // edge
        three_blocks = factor_mode3.shape[1] // edge
        dma = pltpu.SemaphoreType.DMA
        hbm = pl.BlockSpec(memory_space=pltpu.HBM)
        return pl.pallas_call(
            functools.partial(kernel, rows, hi, lo, 16),
            out_shape=jax.ShapeDtypeStruct((rank, IB_DEV * edge), jnp.float32),
            in_specs=[hbm] * 6,
            out_specs=pl.BlockSpec(memory_space=pltpu.VMEM),
            scratch_shapes=[
                pltpu.SMEM((tiles,), jnp.int32),
                pltpu.SMEM((tiles,), jnp.int32),
                pltpu.SMEM((tiles,), jnp.int32),
                pltpu.VMEM(tensor_tiles.shape, jnp.bfloat16),
                pltpu.VMEM((cols * two_blocks, rank, edge), jnp.bfloat16),
                pltpu.VMEM((rows * three_blocks, rank, edge), jnp.bfloat16),
                pltpu.VMEM((tiles // 2, 2 * edge, edge), jnp.bfloat16),
                pltpu.VMEM((tiles // 2, edge, edge), jnp.float32),
                pltpu.VMEM((tiles // 2, edge, edge), jnp.float32),
                pltpu.VMEM((cols, rank + 8, edge), jnp.float32),
                pltpu.VMEM((cols, rank + 8, edge), jnp.float32),
                dma((3,)),
                dma((tiles,)),
                dma((two_blocks + three_blocks,)),
                dma((hi,)), dma((hi,)),
                dma((hi, lo)), dma((hi, lo)),
                dma((hi, lo)), dma((hi, lo)),
                dma((rows,)), dma((rows,)),
                dma((rows,)), dma((rows,)),
                dma((cols,)), dma((cols,)),
            ],
            compiler_params=pltpu.CompilerParams(
                collective_id=0, has_side_effects=True, vmem_limit_bytes=60 * 1024 * 1024
            ),
        )(tile_mode1, tile_mode2, tile_mode3, tensor_tiles, factor_mode2, factor_mode3)

    in_specs = (
        P(("row", "col"), None, None, None),
        P(("row", "col")),
        P(("row", "col")),
        P(("row", "col")),
        P(None, "col"),
        P(None, "row"),
    )
    out_specs = P(None, ("row", "col"))
    return jax.shard_map(body, mesh=mesh, in_specs=in_specs, out_specs=out_specs, check_vma=False)
```

```python
import functools

import jax
import jax.numpy as jnp
from jax import lax
from jax.experimental import pallas as pl
from jax.experimental.pallas import tpu as pltpu
from jax.sharding import PartitionSpec as P

IB_DEV = 8
CORES = 2
MESH = pl.DeviceIdType.MESH
ridge_term = 0.5


def kernel(
    rows, hi, lo, chunk,
    id1_ref, id2_ref, id3_ref, x_ref, f2_ref, f3_ref, out_ref,
    id1, id2, id3, xv, f2g, f3g, weights, scale, sums, slots_a, slots_b, landed_a, landed_b,
    id_sem, x_sem, own_sem, a_send, a_recv, b_send, b_recv, c_send, c_recv,
    d_send, d_recv, e_send, e_recv, s_send, s_recv,
):
    cols = hi * lo
    ny = rows // CORES
    tiles, edge = x_ref.shape[0], x_ref.shape[1]
    rank = f2_ref.shape[0]
    two_blocks = f2_ref.shape[1] // edge
    half = two_blocks // CORES
    three_blocks = f3_ref.shape[1] // edge
    me_r, me_c = lax.axis_index("row"), lax.axis_index("col")
    my_hi, my_lo = me_c // lo, lax.rem(me_c, lo)
    my_y, core = me_r // CORES, lax.rem(me_r, CORES)
    sibling = (me_r + 1 - 2 * core, me_c)

    local = []
    for ref, held, base, count in (
        (f2_ref, f2g, me_c * two_blocks, two_blocks),
        (f3_ref, f3g, me_r * three_blocks, three_blocks),
    ):
        for b in range(count):
            local.append(
                pltpu.make_async_copy(
                    ref.at[:, b * edge : (b + 1) * edge], held.at[base + b], own_sem.at[len(local)]
                )
            )
    loads = [pltpu.make_async_copy(x_ref.at[t], xv.at[t], x_sem.at[t]) for t in range(tiles)]
    ids = [
        pltpu.make_async_copy(ref, held, id_sem.at[n])
        for n, (ref, held) in enumerate(((id1_ref, id1), (id2_ref, id2), (id3_ref, id3)))
    ]
    for copy in local + ids:
        copy.start()

    barrier = pltpu.get_barrier_semaphore()
    partners = [(me_r, lax.rem(me_c + i, cols)) for i in range(1, cols)]
    partners.append(sibling)
    for i in range(1, ny):
        partners.append((lax.rem(my_y + i, ny) * CORES + core, me_c))
    for partner in partners:
        pl.semaphore_signal(barrier, inc=1, device_id=partner, device_id_type=MESH)
    for copy in local:
        copy.wait()
    pl.semaphore_wait(barrier, len(partners))

    sent = []

    def send(src, dst, send_sem, recv_sem, device):
        copy = pltpu.make_async_remote_copy(
            src_ref=src, dst_ref=dst, send_sem=send_sem, recv_sem=recv_sem,
            device_id=device, device_id_type=MESH,
        )
        copy.start()
        sent.append(copy)
        return copy

    def source_col(i, j):
        return lax.rem(my_hi - i + hi, hi) * lo + lax.rem(my_lo - j + lo, lo)

    def piece(col):
        return f2g.at[pl.ds(col * two_blocks + core * half, half)]

    def shard(row):
        return f3g.at[pl.ds(row * three_blocks, three_blocks)]

    mine, mine3 = piece(me_c), shard(me_r)
    a_copies, b_copies, c_copies, d_copies, e_copies = {}, {}, {}, {}, {}
    for i in range(1, hi):
        peer = (me_r, lax.rem(my_hi + i, hi) * lo + my_lo)
        a_copies[i] = send(mine, mine, a_send.at[i], a_recv.at[i], peer)

    def to_lo(i):
        where = piece(source_col(i, 0))
        for j in range(1, lo):
            peer = (me_r, my_hi * lo + lax.rem(my_lo + j, lo))
            b_copies[i, j] = send(where, where, b_send.at[i, j], b_recv.at[i, j], peer)

    def to_sibling(i, j):
        where = piece(source_col(i, j))
        c_copies[i, j] = send(where, where, c_send.at[i, j], c_recv.at[i, j], sibling)

    to_lo(0)
    for i in range(1, ny):
        peer = (lax.rem(my_y + i, ny) * CORES + core, me_c)
        e_copies[i] = send(mine3, mine3, e_send.at[i], e_recv.at[i], peer)
    d_copies[0] = send(mine3, mine3, d_send.at[0], d_recv.at[0], sibling)
    for copy in loads:
        copy.start()
    for i in range(1, hi):
        a_copies[i].wait_recv()
        to_lo(i)
        to_sibling(i, 0)
        for j in range(1, lo):
            b_copies[i - 1, j].wait_recv()
            to_sibling(i - 1, j)
    for i in range(1, ny):
        e_copies[i].wait_recv()
        where = shard(lax.rem(my_y - i + ny, ny) * CORES + core)
        d_copies[i] = send(where, where, d_send.at[i], d_recv.at[i], sibling)
    for j in range(1, lo):
        b_copies[hi - 1, j].wait_recv()
        to_sibling(hi - 1, j)
    for copy in list(c_copies.values()) + list(d_copies.values()):
        copy.wait_recv()
    for copy in ids:
        copy.wait()

    for t in range(tiles):
        pair, side = t // 2, t % 2
        block = f3g[id3[t]].astype(jnp.float32)
        before = jnp.zeros((side * rank, edge), jnp.float32)
        after = jnp.zeros((edge - (side + 1) * rank, edge), jnp.float32)
        stacked = jnp.concatenate(([before] if side else []) + [block, after], axis=0)
        weights[pair, pl.ds(side * edge, edge), :] = stacked.T.astype(jnp.bfloat16)
    for pair in range(tiles // 2):
        blocks = [f2g[id2[t]].astype(jnp.float32) for t in (2 * pair, 2 * pair + 1)]
        blocks.append(jnp.zeros((edge - 2 * rank, edge), jnp.float32))
        scale[pair] = jnp.concatenate(blocks, axis=0).T

    row_blocks = IB_DEV * cols
    half_rank, half_edge = rank // 2, edge // 2
    owners, within = [], []
    for t in range(tiles):
        block = jnp.full((half_rank, edge), id1[t]) - me_r * row_blocks
        owners.append(lax.div(block, jnp.int32(IB_DEV)))
        within.append(lax.rem(block[:1], jnp.int32(IB_DEV)))

    slot_copies = []
    steps = half_edge // chunk
    for part, (slots, landed) in enumerate(((slots_a, landed_a), (slots_b, landed_b))):
        packed = []
        for pair in range(tiles // 2):
            if part == 0:
                loads[2 * pair].wait()
                loads[2 * pair + 1].wait()

            def contract(step, _, pair=pair):
                at = pl.ds(pl.multiple_of(step * chunk, chunk), chunk)
                left = jnp.concatenate(
                    [xv[2 * pair + s, at].reshape(chunk * edge, edge) for s in range(2)], axis=1
                )
                contracted = jnp.dot(left, weights[pair], preferred_element_type=jnp.float32)
                scaled = contracted.reshape(chunk, edge, edge) * scale[pair][None]
                sums[pair, at, :] = jnp.sum(scaled, axis=1)
                return 0

            lax.fori_loop(part * steps, (part + 1) * steps, contract, 0, unroll=2)
            turned = sums[pair, part * half_edge : (part + 1) * half_edge, :].T
            for s in range(2):
                top = turned[s * rank : s * rank + half_rank]
                low = turned[s * rank + half_rank : (s + 1) * rank]
                packed.append(jnp.concatenate([top, low], axis=1))
        for i in list(range(1, cols)) + [0]:
            to = lax.rem(me_c + i, cols)
            values = jnp.zeros((half_rank, edge), jnp.float32)
            for t in range(tiles):
                values = jnp.where(owners[t] == to, packed[t], values)
            target = slots if i else landed
            target[i, :half_rank, :] = values
            if part == 0:
                ident = jnp.full((1, edge), -1, jnp.int32)
                for t in range(tiles):
                    ident = jnp.where(owners[t][:1] == to, within[t], ident)
                target[i, half_rank:, :] = jnp.broadcast_to(ident.astype(jnp.float32), (8, edge))
            if i:
                slot_copies.append(
                    send(
                        slots.at[i], landed.at[i], s_send.at[part, i], s_recv.at[part, i], (me_r, to)
                    )
                )

    def gram(held, count):
        total = jnp.zeros((rank, rank), jnp.float32)
        for base in range(0, count, 16):
            part = jnp.concatenate([held[b] for b in range(base, min(base + 16, count))], axis=1)
            total += lax.dot_general(
                part, part, (((1,), (1,)), ((), ())), preferred_element_type=jnp.float32
            )
        return total

    row_id = lax.broadcasted_iota(jnp.int32, (rank, edge), 0)
    lane_id = lax.broadcasted_iota(jnp.int32, (rank, edge), 1)
    system = gram(f2g, cols * two_blocks) * gram(f3g, rows * three_blocks)
    padded = jnp.concatenate([system, jnp.zeros((rank, edge - rank), jnp.float32)], axis=1)
    padded = padded + jnp.where(lane_id == row_id, ridge_term, 0.0)
    work = padded + jnp.where(lane_id == row_id + rank, 1.0, 0.0)
    for k in range(0, rank, 2):
        first = jnp.broadcast_to(work[:, k : k + 1], (rank, edge))
        second = jnp.broadcast_to(work[:, k + 1 : k + 2], (rank, edge))
        row_a, row_b = work[k : k + 1], work[k + 1 : k + 2]
        inv_a = 1.0 / first[k : k + 1]
        cross = second[k : k + 1]
        factor = first[k + 1 : k + 2] * inv_a
        inv_b = 1.0 / (second[k + 1 : k + 2] - factor * cross)
        new_b = (row_b - factor * row_a) * inv_b
        new_a = (row_a - cross * new_b) * inv_a
        work = work - first * new_a - second * new_b
        work = jnp.where(row_id == k, new_a, jnp.where(row_id == k + 1, new_b, work))
    inverse = work[:, rank : 2 * rank]

    for copy in slot_copies:
        copy.wait_recv()
    for b in range(IB_DEV):
        first = jnp.zeros((half_rank, edge), jnp.float32)
        second = jnp.zeros((half_rank, edge), jnp.float32)
        for i in range(cols):
            hit = landed_a[i, half_rank : half_rank + 1, :] == float(b)
            first += jnp.where(hit, landed_a[i, :half_rank, :], 0.0)
            second += jnp.where(hit, landed_b[i, :half_rank, :], 0.0)
        top = jnp.concatenate([first[:, :half_edge], second[:, :half_edge]], axis=1)
        low = jnp.concatenate([first[:, half_edge:], second[:, half_edge:]], axis=1)
        out_ref[:, b * edge : (b + 1) * edge] = jnp.dot(
            inverse, jnp.concatenate([top, low], axis=0),
            preferred_element_type=jnp.float32, precision=lax.Precision.HIGHEST,
        )
    for copy in sent:
        copy.wait_send()


def solution(mesh):
    rows, cols = mesh.shape["row"], mesh.shape["col"]
    lo = 1
    while 4 * lo * lo <= cols:
        lo *= 2
    hi = cols // lo

    def body(tensor_tiles, tile_mode1, tile_mode2, tile_mode3, factor_mode2, factor_mode3):
        tiles, edge = tensor_tiles.shape[:2]
        rank = factor_mode2.shape[0]
        two_blocks = factor_mode2.shape[1] // edge
        three_blocks = factor_mode3.shape[1] // edge
        dma = pltpu.SemaphoreType.DMA
        hbm = pl.BlockSpec(memory_space=pltpu.HBM)
        return pl.pallas_call(
            functools.partial(kernel, rows, hi, lo, 16),
            out_shape=jax.ShapeDtypeStruct((rank, IB_DEV * edge), jnp.float32),
            in_specs=[hbm] * 6,
            out_specs=pl.BlockSpec(memory_space=pltpu.VMEM),
            scratch_shapes=[
                pltpu.SMEM((tiles,), jnp.int32),
                pltpu.SMEM((tiles,), jnp.int32),
                pltpu.SMEM((tiles,), jnp.int32),
                pltpu.VMEM(tensor_tiles.shape, jnp.bfloat16),
                pltpu.VMEM((cols * two_blocks, rank, edge), jnp.bfloat16),
                pltpu.VMEM((rows * three_blocks, rank, edge), jnp.bfloat16),
                pltpu.VMEM((tiles // 2, 2 * edge, edge), jnp.bfloat16),
                pltpu.VMEM((tiles // 2, edge, edge), jnp.float32),
                pltpu.VMEM((tiles // 2, edge, edge), jnp.float32),
                pltpu.VMEM((cols, rank // 2 + 8, edge), jnp.float32),
                pltpu.VMEM((cols, rank // 2, edge), jnp.float32),
                pltpu.VMEM((cols, rank // 2 + 8, edge), jnp.float32),
                pltpu.VMEM((cols, rank // 2, edge), jnp.float32),
                dma((3,)),
                dma((tiles,)),
                dma((two_blocks + three_blocks,)),
                dma((hi,)), dma((hi,)),
                dma((hi, lo)), dma((hi, lo)),
                dma((hi, lo)), dma((hi, lo)),
                dma((rows,)), dma((rows,)),
                dma((rows,)), dma((rows,)),
                dma((2, cols)), dma((2, cols)),
            ],
            compiler_params=pltpu.CompilerParams(
                collective_id=0, has_side_effects=True, vmem_limit_bytes=60 * 1024 * 1024
            ),
        )(tile_mode1, tile_mode2, tile_mode3, tensor_tiles, factor_mode2, factor_mode3)

    in_specs = (
        P(("row", "col"), None, None, None),
        P(("row", "col")),
        P(("row", "col")),
        P(("row", "col")),
        P(None, "col"),
        P(None, "row"),
    )
    out_specs = P(None, ("row", "col"))
    return jax.shard_map(body, mesh=mesh, in_specs=in_specs, out_specs=out_specs, check_vma=False)
```

```python
import functools

import jax
import jax.numpy as jnp
from jax import lax
from jax.experimental import pallas as pl
from jax.experimental.pallas import tpu as pltpu
from jax.sharding import PartitionSpec as P

IB_DEV = 8
CORES = 2
MESH = pl.DeviceIdType.MESH
ridge_term = 0.5


def kernel(
    rows, hi, lo, chunk,
    id1_ref, id2_ref, id3_ref, x_ref, f2_ref, f3_ref, out_ref,
    id1, id2, id3, xv, f2g, f3g, weights, scale, sums, slots_a, slots_b, landed_a, landed_b,
    id_sem, x_sem, own_sem, a_send, a_recv, b_send, b_recv, c_send, c_recv,
    d_send, d_recv, e_send, e_recv, s_send, s_recv,
):
    cols = hi * lo
    ny = rows // CORES
    tiles, edge = x_ref.shape[0], x_ref.shape[1]
    rank = f2_ref.shape[0]
    two_blocks = f2_ref.shape[1] // edge
    half = two_blocks // CORES
    three_blocks = f3_ref.shape[1] // edge
    me_r, me_c = lax.axis_index("row"), lax.axis_index("col")
    my_hi, my_lo = me_c // lo, lax.rem(me_c, lo)
    my_y, core = me_r // CORES, lax.rem(me_r, CORES)
    sibling = (me_r + 1 - 2 * core, me_c)

    local = []
    for ref, held, base, count in (
        (f2_ref, f2g, me_c * two_blocks, two_blocks),
        (f3_ref, f3g, me_r * three_blocks, three_blocks),
    ):
        for b in range(count):
            local.append(
                pltpu.make_async_copy(
                    ref.at[:, b * edge : (b + 1) * edge], held.at[base + b], own_sem.at[len(local)]
                )
            )
    loads = [pltpu.make_async_copy(x_ref.at[t], xv.at[t], x_sem.at[t]) for t in range(tiles)]
    ids = [
        pltpu.make_async_copy(ref, held, id_sem.at[n])
        for n, (ref, held) in enumerate(((id1_ref, id1), (id2_ref, id2), (id3_ref, id3)))
    ]
    for copy in local + ids:
        copy.start()

    barrier = pltpu.get_barrier_semaphore()
    partners = [(me_r, lax.rem(me_c + i, cols)) for i in range(1, cols)]
    partners.append(sibling)
    for i in range(1, ny):
        partners.append((lax.rem(my_y + i, ny) * CORES + core, me_c))
    for partner in partners:
        pl.semaphore_signal(barrier, inc=1, device_id=partner, device_id_type=MESH)
    for copy in local:
        copy.wait()
    pl.semaphore_wait(barrier, len(partners))

    sent = []

    def send(src, dst, send_sem, recv_sem, device):
        copy = pltpu.make_async_remote_copy(
            src_ref=src, dst_ref=dst, send_sem=send_sem, recv_sem=recv_sem,
            device_id=device, device_id_type=MESH,
        )
        copy.start()
        sent.append(copy)
        return copy

    def source_col(i, j):
        return lax.rem(my_hi - i + hi, hi) * lo + lax.rem(my_lo - j + lo, lo)

    def piece(col):
        return f2g.at[pl.ds(col * two_blocks + core * half, half)]

    def shard(row):
        return f3g.at[pl.ds(row * three_blocks, three_blocks)]

    mine, mine3 = piece(me_c), shard(me_r)
    a_copies, b_copies, c_copies, d_copies, e_copies = {}, {}, {}, {}, {}
    for i in range(1, hi):
        peer = (me_r, lax.rem(my_hi + i, hi) * lo + my_lo)
        a_copies[i] = send(mine, mine, a_send.at[i], a_recv.at[i], peer)

    def to_lo(i):
        where = piece(source_col(i, 0))
        for j in range(1, lo):
            peer = (me_r, my_hi * lo + lax.rem(my_lo + j, lo))
            b_copies[i, j] = send(where, where, b_send.at[i, j], b_recv.at[i, j], peer)

    def to_sibling(i, j):
        where = piece(source_col(i, j))
        c_copies[i, j] = send(where, where, c_send.at[i, j], c_recv.at[i, j], sibling)

    to_lo(0)
    for i in range(1, ny):
        peer = (lax.rem(my_y + i, ny) * CORES + core, me_c)
        e_copies[i] = send(mine3, mine3, e_send.at[i], e_recv.at[i], peer)
    d_copies[0] = send(mine3, mine3, d_send.at[0], d_recv.at[0], sibling)
    for copy in loads:
        copy.start()
    for i in range(1, hi):
        a_copies[i].wait_recv()
        to_lo(i)
        to_sibling(i, 0)
        for j in range(1, lo):
            b_copies[i - 1, j].wait_recv()
            to_sibling(i - 1, j)
    for i in range(1, ny):
        e_copies[i].wait_recv()
        where = shard(lax.rem(my_y - i + ny, ny) * CORES + core)
        d_copies[i] = send(where, where, d_send.at[i], d_recv.at[i], sibling)
    for j in range(1, lo):
        b_copies[hi - 1, j].wait_recv()
        to_sibling(hi - 1, j)
    for copy in list(c_copies.values()) + list(d_copies.values()):
        copy.wait_recv()
    for copy in ids:
        copy.wait()

    for t in range(tiles):
        pair, side = t // 2, t % 2
        block = f3g[id3[t]].astype(jnp.float32)
        before = jnp.zeros((side * rank, edge), jnp.float32)
        after = jnp.zeros((edge - (side + 1) * rank, edge), jnp.float32)
        stacked = jnp.concatenate(([before] if side else []) + [block, after], axis=0)
        weights[pair, pl.ds(side * edge, edge), :] = stacked.T.astype(jnp.bfloat16)
    for pair in range(tiles // 2):
        blocks = [f2g[id2[t]].astype(jnp.float32) for t in (2 * pair, 2 * pair + 1)]
        blocks.append(jnp.zeros((edge - 2 * rank, edge), jnp.float32))
        scale[pair] = jnp.concatenate(blocks, axis=0).T

    row_blocks = IB_DEV * cols
    half_rank, half_edge = rank // 2, edge // 2
    owners, within = [], []
    for t in range(tiles):
        block = jnp.full((half_rank, edge), id1[t]) - me_r * row_blocks
        owners.append(lax.div(block, jnp.int32(IB_DEV)))
        within.append(lax.rem(block[:1], jnp.int32(IB_DEV)))

    row_id = lax.broadcasted_iota(jnp.int32, (rank, edge), 0)
    lane_id = lax.broadcasted_iota(jnp.int32, (rank, edge), 1)

    def gram_term(held, base, count):
        part = jnp.concatenate([held[b] for b in range(base, min(base + 16, count))], axis=1)
        return lax.dot_general(
            part, part, (((1,), (1,)), ((), ())), preferred_element_type=jnp.float32
        )

    two_count, three_count = cols * two_blocks, rows * three_blocks
    terms = [(0, f2g, base, two_count) for base in range(0, two_count, 16)]
    terms += [(1, f3g, base, three_count) for base in range(0, three_count, 16)]

    def first_work(grams):
        system = grams[0] * grams[1]
        work = jnp.concatenate([system, jnp.zeros((rank, edge - rank), jnp.float32)], axis=1)
        work = work + jnp.where(lane_id == row_id, ridge_term, 0.0)
        return work + jnp.where(lane_id == row_id + rank, 1.0, 0.0)

    def eliminate(work, k):
        first = jnp.broadcast_to(work[:, k : k + 1], (rank, edge))
        second = jnp.broadcast_to(work[:, k + 1 : k + 2], (rank, edge))
        row_a, row_b = work[k : k + 1], work[k + 1 : k + 2]
        inv_a = 1.0 / first[k : k + 1]
        cross = second[k : k + 1]
        factor = first[k + 1 : k + 2] * inv_a
        inv_b = 1.0 / (second[k + 1 : k + 2] - factor * cross)
        new_b = (row_b - factor * row_a) * inv_b
        new_a = (row_a - cross * new_b) * inv_a
        work = work - first * new_a - second * new_b
        return jnp.where(row_id == k, new_a, jnp.where(row_id == k + 1, new_b, work))

    slot_copies = []
    steps = half_edge // chunk
    calls = steps * (tiles // 2)
    grams = [jnp.zeros((rank, rank), jnp.float32)] * 2
    work = None
    for part, (slots, landed) in enumerate(((slots_a, landed_a), (slots_b, landed_b))):
        packed = []
        if part == 1:
            work = first_work(grams)
        for pair in range(tiles // 2):
            if part == 0:
                loads[2 * pair].wait()
                loads[2 * pair + 1].wait()

            for step in range(steps):
                at = pl.ds((part * steps + step) * chunk, chunk)
                left = jnp.concatenate(
                    [xv[2 * pair + s, at].reshape(chunk * edge, edge) for s in range(2)], axis=1
                )
                contracted = jnp.dot(left, weights[pair], preferred_element_type=jnp.float32)
                scaled = contracted.reshape(chunk, edge, edge) * scale[pair][None]
                sums[pair, at, :] = jnp.sum(scaled, axis=1)
                call = pair * steps + step
                if part == 0:
                    for which, held, base, count in terms[call::calls]:
                        grams[which] = grams[which] + gram_term(held, base, count)
                else:
                    pivots = rank // 2
                    for k in range(pivots * call // calls, pivots * (call + 1) // calls):
                        work = eliminate(work, 2 * k)
            turned = sums[pair, part * half_edge : (part + 1) * half_edge, :].T
            for s in range(2):
                top = turned[s * rank : s * rank + half_rank]
                low = turned[s * rank + half_rank : (s + 1) * rank]
                packed.append(jnp.concatenate([top, low], axis=1))
        for i in list(range(1, cols)) + [0]:
            to = lax.rem(me_c + i, cols)
            values = jnp.zeros((half_rank, edge), jnp.float32)
            for t in range(tiles):
                values = jnp.where(owners[t] == to, packed[t], values)
            target = slots if i else landed
            target[i, :half_rank, :] = values
            if part == 0:
                ident = jnp.full((1, edge), -1, jnp.int32)
                for t in range(tiles):
                    ident = jnp.where(owners[t][:1] == to, within[t], ident)
                target[i, half_rank:, :] = jnp.broadcast_to(ident.astype(jnp.float32), (8, edge))
            if i:
                slot_copies.append(
                    send(
                        slots.at[i], landed.at[i], s_send.at[part, i], s_recv.at[part, i], (me_r, to)
                    )
                )

    inverse = work[:, rank : 2 * rank]
    for copy in slot_copies:
        copy.wait_recv()
    right = []
    for b in range(IB_DEV):
        first = jnp.zeros((half_rank, edge), jnp.float32)
        second = jnp.zeros((half_rank, edge), jnp.float32)
        for i in range(cols):
            hit = landed_a[i, half_rank : half_rank + 1, :] == float(b)
            first += jnp.where(hit, landed_a[i, :half_rank, :], 0.0)
            second += jnp.where(hit, landed_b[i, :half_rank, :], 0.0)
        top = jnp.concatenate([first[:, :half_edge], second[:, :half_edge]], axis=1)
        low = jnp.concatenate([first[:, half_edge:], second[:, half_edge:]], axis=1)
        right.append(jnp.concatenate([top, low], axis=0))
    out_ref[...] = jnp.dot(
        inverse, jnp.concatenate(right, axis=1),
        preferred_element_type=jnp.float32, precision=lax.Precision.HIGHEST,
    )
    for copy in sent:
        copy.wait_send()


def solution(mesh):
    rows, cols = mesh.shape["row"], mesh.shape["col"]
    lo = 1
    while 4 * lo * lo <= cols:
        lo *= 2
    hi = cols // lo

    def body(tensor_tiles, tile_mode1, tile_mode2, tile_mode3, factor_mode2, factor_mode3):
        tiles, edge = tensor_tiles.shape[:2]
        rank = factor_mode2.shape[0]
        two_blocks = factor_mode2.shape[1] // edge
        three_blocks = factor_mode3.shape[1] // edge
        dma = pltpu.SemaphoreType.DMA
        hbm = pl.BlockSpec(memory_space=pltpu.HBM)
        return pl.pallas_call(
            functools.partial(kernel, rows, hi, lo, 16),
            out_shape=jax.ShapeDtypeStruct((rank, IB_DEV * edge), jnp.float32),
            in_specs=[hbm] * 6,
            out_specs=pl.BlockSpec(memory_space=pltpu.VMEM),
            scratch_shapes=[
                pltpu.SMEM((tiles,), jnp.int32),
                pltpu.SMEM((tiles,), jnp.int32),
                pltpu.SMEM((tiles,), jnp.int32),
                pltpu.VMEM(tensor_tiles.shape, jnp.bfloat16),
                pltpu.VMEM((cols * two_blocks, rank, edge), jnp.bfloat16),
                pltpu.VMEM((rows * three_blocks, rank, edge), jnp.bfloat16),
                pltpu.VMEM((tiles // 2, 2 * edge, edge), jnp.bfloat16),
                pltpu.VMEM((tiles // 2, edge, edge), jnp.float32),
                pltpu.VMEM((tiles // 2, edge, edge), jnp.float32),
                pltpu.VMEM((cols, rank // 2 + 8, edge), jnp.float32),
                pltpu.VMEM((cols, rank // 2, edge), jnp.float32),
                pltpu.VMEM((cols, rank // 2 + 8, edge), jnp.float32),
                pltpu.VMEM((cols, rank // 2, edge), jnp.float32),
                dma((3,)),
                dma((tiles,)),
                dma((two_blocks + three_blocks,)),
                dma((hi,)), dma((hi,)),
                dma((hi, lo)), dma((hi, lo)),
                dma((hi, lo)), dma((hi, lo)),
                dma((rows,)), dma((rows,)),
                dma((rows,)), dma((rows,)),
                dma((2, cols)), dma((2, cols)),
            ],
            compiler_params=pltpu.CompilerParams(
                collective_id=0, has_side_effects=True, vmem_limit_bytes=60 * 1024 * 1024
            ),
        )(tile_mode1, tile_mode2, tile_mode3, tensor_tiles, factor_mode2, factor_mode3)

    in_specs = (
        P(("row", "col"), None, None, None),
        P(("row", "col")),
        P(("row", "col")),
        P(("row", "col")),
        P(None, "col"),
        P(None, "row"),
    )
    out_specs = P(None, ("row", "col"))
    return jax.shard_map(body, mesh=mesh, in_specs=in_specs, out_specs=out_specs, check_vma=False)
```
